32 devices in a mesh: batch: 8 (over z, y), tile: 2 (over x), cuts: 2 (over core).
Axes of the slice: x: 2, y: 2, z: 4, core: 2. Of those that a mesh axis runs over, the one named last changes fastest.
Arguments:
- objects: float32 [2, 16, 2, 256, 256], P('cuts', 'tile'), may hold values from -5 to 5
- probe: float32 [4, 2, 256, 256], replicated, may hold values from -5 to 5
- measured: float32 [16, 256, 256], P(('batch', 'tile')), may hold values from 0 to 6
- send_list: int32 [8, 2, 2], P('batch', 'tile'), may hold values from 0 to 7
- corner_slot: int32 [16, 4], P(('batch', 'tile')), may hold values from 0 to 1
- offsets: int32 [16, 2], P(('batch', 'tile')), may hold values from 0 to 255
Outputs:
- new_objects: float32 [2, 16, 2, 256, 256], P('cuts', 'tile')
- new_probe: float32 [4, 2, 256, 256], P('cuts', None, 'tile')
The draws below stay inside these ranges and needn't reach their ends.
Inputs may be any that keep to these rules, and one draw needn't show every extreme that they name: `send_list`: local tile indices of the owner. `corner_slot`: indices of the owner within the group.
All inputs are finite; a program needn't handle non-finite values.
Results may differ from the reference program's by a relative error of at most 0.0003.
Values sent between devices are 32-bit elements; how exact they have to be, the bound alone decides.
A program may use at most 128 MiB of HBM per device.

```python
import math
import jax
import jax.numpy as jnp
from jax import lax

PATCH = 256
MODES = 4
TILES_DEV = 8
POS_DEV = 1
SLICES = 2
TILES = 16
POSITIONS = 16
N_BATCH = 8
N_TILE = 2


def touch_ends(array, key, smallest, largest):
    longest = array.shape.index(max(array.shape))
    spots = []
    for shift in (0, 1):
        where = [jax.random.randint(jax.random.fold_in(key, axis), (), 0, length) for axis, length in enumerate(array.shape)]
        where[longest] = (where[longest] + shift) % array.shape[longest]
        spots.append(tuple(where))
    return array.at[spots[0]].set(smallest).at[spots[1]].set(largest)


def levels(own_key, extent, cuts, smallest, high):
    loudness = 1.0
    for axis_at, shards_of in cuts:
        heights = jax.random.uniform(jax.random.fold_in(jax.random.fold_in(own_key, 6), axis_at), (shards_of,), jnp.float32, smallest / len(cuts), high / len(cuts))
        loudness = loudness * jnp.repeat(jnp.exp(heights), extent[axis_at] // shards_of).reshape((-1,) + (1,) * (len(extent) - 1 - axis_at))
    return loudness


def normal_values(rng, extent, width, reach, shards=(), kind=jnp.bfloat16):
    values = jax.random.normal(rng, extent, jnp.float32) * width
    if len(shards) > 0:
        values = levels(rng, extent, shards, -0.22, 0.18) * values
    return jnp.clip(values, min=-reach, max=reach).astype(kind)


def setup_inputs(seed: int = 0) -> dict:
    keys = jax.random.split(jax.random.key(seed), 7)
    objects = normal_values(keys[0], (SLICES, TILES, 2, PATCH, PATCH), 0.8, 5.0, ((0, 2), (1, 2)), jnp.float32)
    probe = normal_values(keys[1], (MODES, 2, PATCH, PATCH), 0.5, 5.0, (), jnp.float32)
    measured = jnp.clip(6.0 * jax.random.uniform(keys[2], (POSITIONS, PATCH, PATCH), jnp.float32) ** levels(keys[2], (POSITIONS, PATCH, PATCH), ((0, 16),), -0.2, 0.2), 0.0, 6.0)
    send_list = touch_ends(jax.random.randint(keys[3], (N_BATCH, N_TILE, N_TILE), 0, TILES_DEV), jax.random.fold_in(keys[3], 1), 0, TILES_DEV - 1).astype(jnp.int32)
    corner_slot = touch_ends(jax.random.randint(keys[4], (POSITIONS, 4), 0, N_TILE), jax.random.fold_in(keys[4], 1), 0, N_TILE - 1).astype(jnp.int32)
    offsets = touch_ends(jax.random.randint(keys[5], (POSITIONS, 2), 0, PATCH), jax.random.fold_in(keys[5], 1), 0, PATCH - 1).astype(jnp.int32)
    return {"objects": objects, "probe": probe, "measured": measured, "send_list": send_list, "corner_slot": corner_slot, "offsets": offsets}


OBJECT_RATE = 0.02
PROBE_RATE = 0.05

def chirp_factor(length, dtype):
    counter = jnp.arange(length, dtype=jnp.int32)
    signed = jnp.where(counter < length // 2, counter, counter - length)
    quadric = signed * signed % (2 * length)
    angle = math.pi / length * quadric.astype(dtype)
    single = lax.complex(jnp.cos(angle), -jnp.sin(angle))
    return single[:, None] * single[None, :]

def reference(objects, probe, measured, send_list, corner_slot, offsets):
    length = PATCH
    tile_field = lax.complex(objects[:, :, 0], objects[:, :, 1])
    probe_field = lax.complex(probe[:, 0], probe[:, 1])
    transfer = chirp_factor(length, objects.dtype)
    batch_place = jnp.arange(POSITIONS, dtype=jnp.int32) // POS_DEV
    zero_index = jnp.zeros((), jnp.int32)

    def one_position(running, entries):
        tile_grad, probe_grad = running
        intensity_data, slot_row, start_cell, device_place = entries
        start_row = start_cell[0].astype(jnp.int32)
        start_col = start_cell[1].astype(jnp.int32)
        group_index = device_place // N_TILE
        member_index = device_place % N_TILE
        local_index = send_list[group_index, slot_row, member_index]
        tile_ids = (slot_row * TILES_DEV + local_index).astype(jnp.int32)
        corner_tiles = tile_field[:, tile_ids]
        region = corner_tiles.reshape(SLICES, 2, 2, length, length).transpose(0, 1, 3, 2, 4)
        region = region.reshape(SLICES, 2 * length, 2 * length)
        patch_pair = lax.dynamic_slice(region, (zero_index, start_row, start_col), (SLICES, length, length))
        first_patch = patch_pair[0]
        second_patch = patch_pair[1]
        spread = jnp.fft.ifft2(jnp.fft.fft2(probe_field * first_patch[None]) * transfer)
        far_wave = jnp.fft.fft2(second_patch[None] * spread, norm='ortho')
        intensity = lax.optimization_barrier(jnp.sum(jnp.real(far_wave) ** 2 + jnp.imag(far_wave) ** 2, axis=0))
        residual = intensity - intensity_data
        returned = jnp.fft.ifft2(residual[None] * far_wave, norm='ortho')
        grad_second = lax.optimization_barrier(jnp.sum(jnp.conj(spread) * returned, axis=0))
        spread_back = jnp.fft.ifft2(jnp.fft.fft2(jnp.conj(second_patch)[None] * returned) * jnp.conj(transfer))
        grad_first = lax.optimization_barrier(jnp.sum(jnp.conj(probe_field) * spread_back, axis=0))
        probe_grad = probe_grad + jnp.conj(first_patch)[None] * spread_back
        grad_pair = jnp.stack([grad_first, grad_second])
        zero_region = jnp.zeros((SLICES, 2 * length, 2 * length), grad_pair.dtype)
        region_grad = lax.dynamic_update_slice(zero_region, grad_pair, (zero_index, start_row, start_col))
        corner_grad = region_grad.reshape(SLICES, 2, length, 2, length).transpose(0, 1, 3, 2, 4)
        corner_grad = corner_grad.reshape(SLICES, 4, length, length)
        tile_grad = tile_grad.at[:, tile_ids].add(corner_grad)
        return ((tile_grad, probe_grad), None)
    start_state = (jnp.zeros_like(tile_field), jnp.zeros_like(probe_field))
    final_state, unused_output = lax.scan(one_position, start_state, (measured, corner_slot, offsets, batch_place))
    tile_grad, probe_grad = final_state
    new_tiles = tile_field - OBJECT_RATE * tile_grad
    new_modes = probe_field - PROBE_RATE / math.sqrt(POSITIONS) * probe_grad
    new_objects = jnp.stack([jnp.real(new_tiles), jnp.imag(new_tiles)], axis=2)
    new_probe = jnp.stack([jnp.real(new_modes), jnp.imag(new_modes)], axis=1)
    return (new_objects, new_probe)
```

```python
import math

import jax
import jax.numpy as jnp
import numpy as np
from jax import lax
from jax.sharding import PartitionSpec as P

HIGH = lax.Precision.HIGH
OBJECT_RATE = 0.02
PROBE_RATE = 0.05


def transform_tables(length):
    counter = np.arange(length)
    wave = np.exp(-2j * np.pi / length * (counter[:, None] * counter[None, :] % length))
    signed = np.where(counter < length // 2, counter, counter - length)
    chirp = np.exp(-1j * np.pi / length * (signed * signed % (2 * length)))
    fresnel = (np.conj(wave) * chirp[None, :]) @ wave / length
    unitary = wave / math.sqrt(length)
    as_pair = lambda m: (np.real(m).astype(np.float32), np.imag(m).astype(np.float32))
    return as_pair(fresnel), as_pair(unitary)


def conjugate(matrix):
    return (matrix[0], -matrix[1])


def complex_times(a, b):
    return (a[0] * b[0] - a[1] * b[1], a[0] * b[1] + a[1] * b[0])


def conj_times(a, b):
    return (a[0] * b[0] + a[1] * b[1], a[0] * b[1] - a[1] * b[0])


def apply_both(matrix, field):
    re, im = matrix
    left = np.concatenate([np.concatenate([re, -im], 1), np.concatenate([im, re], 1)], 0)
    right = np.concatenate([np.concatenate([re, im], 1), np.concatenate([-im, re], 1)], 0)
    length = re.shape[0]
    stacked = jnp.concatenate([field[0], field[1]], axis=-1)
    wide = jnp.einsum("mjk,kl->mjl", stacked, right, precision=HIGH)
    tall = jnp.concatenate([wide[..., :length], wide[..., length:]], axis=-2)
    done = jnp.einsum("jk,mkl->mjl", left, tall, precision=HIGH)
    return (done[:, :length], done[:, length:])


def swap(value, axis):
    return lax.ppermute(value, axis, [(0, 1), (1, 0)])


def local(objects, probe, measured, send_list, corner_slot, offsets):
    length = probe.shape[-1]
    half = probe.shape[0] // 2
    groups = lax.axis_size("tile")
    row_block = length // groups
    cut = lax.axis_index("cuts")
    fresnel, farfield = transform_tables(length)
    owned = objects[0]
    pick = send_list[0, 0]
    outgoing = jnp.take(owned, pick, axis=0)
    arrived = lax.all_to_all(outgoing, "tile", split_axis=0, concat_axis=0, tiled=True)

    y0, x0 = offsets[0, 0], offsets[0, 1]
    cells = jnp.arange(length, dtype=jnp.int32)
    low_row = (cells < y0)[:, None]
    low_col = (cells < x0)[None, :]
    slots = corner_slot[0]
    slot_plane = jnp.where(
        low_row, jnp.where(low_col, slots[3], slots[2]), jnp.where(low_col, slots[1], slots[0])
    )
    tile_own = arrived[0]
    for o in range(1, groups):
        tile_own = jnp.where(slot_plane == o, arrived[o], tile_own)
    tile_other = swap(tile_own, "cuts")
    first = cut == 0
    t0 = jnp.where(first, tile_own, tile_other)
    t1 = jnp.where(first, tile_other, tile_own)
    t0 = (t0[0][None], t0[1][None])
    t1 = (t1[0][None], t1[1][None])
    my_probe = lax.dynamic_slice_in_dim(probe, cut * half, half, 0)
    rolled = jnp.roll(my_probe, (y0, x0), axis=(2, 3))
    p = (rolled[:, 0], rolled[:, 1])

    phi = apply_both(fresnel, complex_times(p, t0))
    psi = apply_both(farfield, complex_times(t1, phi))
    part = jnp.sum(psi[0] * psi[0] + psi[1] * psi[1], axis=0)
    resid = (part + swap(part, "cuts")) - measured[0]
    chi = apply_both(conjugate(farfield), (resid[None] * psi[0], resid[None] * psi[1]))
    g1 = jnp.stack([jnp.sum(v, axis=0) for v in conj_times(phi, chi)])
    zeta = apply_both(conjugate(fresnel), conj_times(t1, chi))
    g0 = jnp.stack([jnp.sum(v, axis=0) for v in conj_times(p, zeta)])
    probe_term = jnp.stack(conj_times(t0, zeta), axis=1)
    probe_term = jnp.roll(probe_term, (-y0, -x0), axis=(2, 3))
    grad = jnp.where(first, g0, g1) + swap(jnp.where(first, g1, g0), "cuts")

    slot_grads = jnp.stack([jnp.where(slot_plane == o, grad, 0.0) for o in range(groups)])
    probe_blocks = probe_term.reshape(half * 2, groups, row_block, length)
    returned = lax.all_to_all(slot_grads, "tile", split_axis=0, concat_axis=0, tiled=True)
    pieces = lax.all_to_all(probe_blocks, "tile", split_axis=1, concat_axis=1, tiled=True)
    probe_rows = jnp.sum(pieces, axis=1).reshape(half, 2, row_block, length)
    tile_count = owned.shape[0]
    tile_ids = jnp.arange(tile_count, dtype=jnp.int32)[:, None, None, None]
    tile_term = jnp.where(pick[0] == tile_ids, returned[0][None], 0.0)
    for s in range(1, groups):
        tile_term = tile_term + jnp.where(pick[s] == tile_ids, returned[s][None], 0.0)
    tile_total, probe_total = lax.psum((tile_term, probe_rows), "batch")
    new_objects = objects - OBJECT_RATE * tile_total[None]
    row_start = lax.axis_index("tile") * row_block
    own_probe = lax.dynamic_slice_in_dim(my_probe, row_start, row_block, 2)
    position_total = lax.axis_size("batch") * groups
    new_probe = own_probe - PROBE_RATE / math.sqrt(position_total) * probe_total
    return (new_objects, new_probe)


def solution(mesh):
    in_specs = (
        P("cuts", "tile", None, None, None),
        P(),
        P(("batch", "tile"), None, None),
        P("batch", "tile", None),
        P(("batch", "tile"), None),
        P(("batch", "tile"), None),
    )
    out_specs = (P("cuts", "tile", None, None, None), P("cuts", None, "tile", None))
    return jax.shard_map(local, mesh=mesh, in_specs=in_specs, out_specs=out_specs, check_vma=False)
```

```python
import functools
import math

import jax
import jax.numpy as jnp
import numpy as np
from jax import lax
from jax.experimental import pallas as pl
from jax.experimental.pallas import tpu as pltpu
from jax.sharding import PartitionSpec as P

EXACT = lax.Precision.HIGHEST
OBJECT_RATE = 0.02
PROBE_RATE = 0.05


def transform_tables(length):
    counter = np.arange(length)
    wave = np.exp(-2j * np.pi / length * (counter[:, None] * counter[None, :] % length))
    signed = np.where(counter < length // 2, counter, counter - length)
    chirp = np.exp(-1j * np.pi / length * (signed * signed % (2 * length)))
    fresnel = (np.conj(wave) * chirp[None, :]) @ wave / length
    unitary = wave / math.sqrt(length)
    as_pair = lambda m: (np.real(m).astype(np.float32), np.imag(m).astype(np.float32))
    return as_pair(fresnel), as_pair(unitary)


def conjugate(matrix):
    return (matrix[0], -matrix[1])


def complex_times(a, b):
    return (a[0] * b[0] - a[1] * b[1], a[0] * b[1] + a[1] * b[0])


def conj_times(a, b):
    return (a[0] * b[0] + a[1] * b[1], a[0] * b[1] - a[1] * b[0])


def apply_both(matrix, field):
    re, im = matrix
    left = np.concatenate([np.concatenate([re, -im], 1), np.concatenate([im, re], 1)], 0)
    right = np.concatenate([np.concatenate([re, im], 1), np.concatenate([-im, re], 1)], 0)
    length = re.shape[0]
    stacked = jnp.concatenate([field[0], field[1]], axis=-1)
    wide = jnp.einsum("mjk,kl->mjl", stacked, right, precision=EXACT)
    tall = jnp.concatenate([wide[..., :length], wide[..., length:]], axis=-2)
    done = jnp.einsum("jk,mkl->mjl", left, tall, precision=EXACT)
    return (done[:, :length], done[:, length:])


def swap(value, axis):
    return lax.ppermute(value, axis, [(0, 1), (1, 0)])


MESH = pl.DeviceIdType.MESH


def reduce_kernel(
    batches, groups, rows, chunks,
    msg, prb, own_obj, own_prb, out_obj, out_prb,
    got, px, ps, py, obj, prn,
    g_send, g_recv, f_send, f_recv, x_send, x_recv, y_send, y_recv,
    a_send, a_recv, b_send, b_recv, l_sem,
):
    me, mine = lax.axis_index("batch"), lax.axis_index("tile")
    depth = batches // 2
    pair = me + 1 - 2 * (me % 2)
    tiles = own_obj.shape[0] // 2
    behind = lambda d: (me + batches - d) % batches

    barrier = pltpu.get_barrier_semaphore()
    for d in range(1, batches):
        pl.semaphore_signal(
            barrier, inc=1, device_id={"batch": (me + d) % batches}, device_id_type=MESH
        )
    for e in range(1, groups):
        pl.semaphore_signal(
            barrier, inc=1, device_id={"tile": (mine + e) % groups}, device_id_type=MESH
        )
    pl.semaphore_wait(barrier, batches + groups - 2)

    def send(src, dst, sems, place, target):
        copy = pltpu.make_async_remote_copy(
            src_ref=src, dst_ref=dst, send_sem=sems[0].at[place], recv_sem=sems[1].at[place],
            device_id=target, device_id_type=MESH,
        )
        copy.start()
        return copy

    to_batch = lambda d: {"batch": (me + d) % batches}
    to_tile = lambda e: {"tile": (mine + e) % groups}
    sent = []
    first = {}
    halves = []
    for e in range(1, groups):
        halves.append(
            send(prb.at[(mine + e) % groups], px.at[e], (x_send, x_recv), e, to_tile(e))
        )
    for d in range(1, batches):
        first[d] = send(
            msg.at[(me + d) % batches], got.at[0, d], (g_send, g_recv), d, to_batch(d)
        )
    got[0, 0] = msg[me]
    forwards = []

    def forward(d):
        for e in range(1, groups):
            forwards.append(
                send(got.at[0, d], got.at[e, d], (f_send, f_recv), e * batches + d, to_tile(e))
            )

    forward(0)
    for copy in halves:
        copy.wait()

    def add_probe(b, carry):
        total = prb[mine, b]
        for e in range(1, groups):
            total = total + px[e, b]
        ps[b] = total
        return carry

    lax.fori_loop(0, batches, add_probe, 0)
    probe_sends = [
        send(ps.at[(me + d) % batches], py.at[d], (y_send, y_recv), d, to_batch(d))
        for d in range(1, batches)
    ]
    for d in range(1, batches):
        first[d].wait_recv()
        forward(d)
    for copy in forwards:
        copy.wait()

    mine_f = mine.astype(jnp.float32)
    strips = rows // 8

    def add_strip(i, carry):
        plane, strip = i // strips, i % strips
        start = pl.multiple_of(i * 8, 8)
        row = (lax.broadcasted_iota(jnp.int32, (8, 256), 0) + strip * 8).astype(jnp.float32)
        sums = [jnp.zeros((8, 256), jnp.float32) for _ in range(tiles)]
        for d in range(batches):
            for e in range(groups):
                upper = got[e, d, pl.ds(2 * rows, 1), :]
                lower = got[e, d, pl.ds(2 * rows + 1, 1), :]
                edge = got[e, d, pl.ds(2 * rows + 2, 1), :]
                place = got[0, d, pl.ds(2 * rows + 3 + e, 1), :]
                slot = jnp.where(row < edge, lower, upper)
                value = jnp.where(slot == mine_f, got[e, d, pl.ds(start, 8), :], 0.0)
                for j in range(tiles):
                    sums[j] = sums[j] + jnp.where(place == float(j), value, 0.0)
        spot = pl.multiple_of(strip * 8, 8)
        for j in range(tiles):
            obj[2 * j + plane, pl.ds(spot, 8), :] = (
                own_obj[2 * j + plane, pl.ds(spot, 8), :] - OBJECT_RATE * sums[j]
            )
        return carry

    lax.fori_loop(0, 2 * strips, add_strip, 0)

    locals_ = [pltpu.make_async_copy(obj, out_obj.at[:, me], l_sem.at[0])]
    locals_[0].start()
    part = 2 * tiles // chunks
    pieces = [pl.ds(q * part, part) for q in range(chunks)]
    arriving = {}

    def gather_start(q, src, dst):
        base = q * depth
        arriving[q, 0] = send(src, dst, (a_send, a_recv), base, {"batch": pair})
        for k in range(1, depth):
            arriving[q, k] = send(src, dst, (a_send, a_recv), base + k, to_batch(2 * k))

    for q in range(chunks):
        gather_start(q, obj.at[pieces[q]], out_obj.at[pieces[q], me])

    for copy in probe_sends:
        copy.wait()
    total = ps[me]
    for d in range(1, batches):
        total = total + py[d]
    prn[...] = own_prb[...] - PROBE_RATE / math.sqrt(batches * groups) * total
    locals_.append(pltpu.make_async_copy(prn, out_prb.at[me], l_sem.at[1]))
    locals_[1].start()
    gather_start(chunks, prn, out_prb.at[me])

    relays = []
    for q in range(chunks + 1):
        for k in range(1, depth):
            arriving[q, k].wait_recv()
            b = behind(2 * k)
            ref = out_obj.at[pieces[q], b] if q < chunks else out_prb.at[b]
            relays.append(send(ref, ref, (b_send, b_recv), q * depth + k, {"batch": pair}))
    for q in range(chunks + 1):
        arriving[q, 0].wait_recv()
    for copy in relays:
        copy.wait()
    for copy in arriving.values():
        copy.wait_send()
    for d in range(1, batches):
        first[d].wait_send()
    for copy in locals_:
        copy.wait()


def reduce_and_gather(messages, probe_blocks, own_objects, own_probe, batches, groups, rows):
    length = messages.shape[-1]
    chunks = 4
    depth = batches // 2
    dma = pltpu.SemaphoreType.DMA
    f32 = jnp.float32
    probe_rows = own_probe.shape[0]
    vmem = pl.BlockSpec(memory_space=pltpu.VMEM)
    return pl.pallas_call(
        functools.partial(reduce_kernel, batches, groups, rows, chunks),
        out_shape=(
            jax.ShapeDtypeStruct((own_objects.shape[0], batches, rows, length), f32),
            jax.ShapeDtypeStruct((batches, probe_rows, length), f32),
        ),
        in_specs=[vmem] * 4,
        out_specs=(pl.BlockSpec(memory_space=pl.ANY), pl.BlockSpec(memory_space=pl.ANY)),
        scratch_shapes=[
            pltpu.VMEM((groups, batches) + messages.shape[1:], f32),
            pltpu.VMEM((groups, batches, probe_rows, length), f32),
            pltpu.VMEM((batches, probe_rows, length), f32),
            pltpu.VMEM((batches, probe_rows, length), f32),
            pltpu.VMEM(own_objects.shape, f32),
            pltpu.VMEM(own_probe.shape, f32),
            dma((batches,)), dma((batches,)),
            dma((groups * batches,)), dma((groups * batches,)),
            dma((groups,)), dma((groups,)),
            dma((batches,)), dma((batches,)),
            dma(((chunks + 1) * depth,)), dma(((chunks + 1) * depth,)),
            dma(((chunks + 1) * depth,)), dma(((chunks + 1) * depth,)),
            dma((2,)),
        ],
        compiler_params=pltpu.CompilerParams(
            collective_id=0, has_side_effects=True, vmem_limit_bytes=40 * 1024 * 1024
        ),
        cost_estimate=pl.CostEstimate(flops=20_000_000, bytes_accessed=12_000_000, transcendentals=0),
    )(messages, probe_blocks, own_objects, own_probe)


def local(objects, probe, measured, send_list, corner_slot, offsets):
    length = probe.shape[-1]
    half = probe.shape[0] // 2
    groups = lax.axis_size("tile")
    batches = lax.axis_size("batch")
    row_block = length // groups
    cut = lax.axis_index("cuts")
    fresnel, farfield = transform_tables(length)
    owned = objects[0]
    pick = send_list[0, 0]
    outgoing = jnp.take(owned, pick, axis=0)
    arrived = lax.all_to_all(outgoing, "tile", split_axis=0, concat_axis=0, tiled=True)

    y0, x0 = offsets[0, 0], offsets[0, 1]
    cells = jnp.arange(length, dtype=jnp.int32)
    low_row = (cells < y0)[:, None]
    low_col = (cells < x0)[None, :]
    slots = corner_slot[0]
    slot_plane = jnp.where(
        low_row, jnp.where(low_col, slots[3], slots[2]), jnp.where(low_col, slots[1], slots[0])
    )
    tile_own = arrived[0]
    for o in range(1, groups):
        tile_own = jnp.where(slot_plane == o, arrived[o], tile_own)
    tile_other = swap(tile_own, "cuts")
    first = cut == 0
    t0 = jnp.where(first, tile_own, tile_other)
    t1 = jnp.where(first, tile_other, tile_own)
    t0 = (t0[0][None], t0[1][None])
    t1 = (t1[0][None], t1[1][None])
    my_probe = lax.dynamic_slice_in_dim(probe, cut * half, half, 0)
    rolled = jnp.roll(my_probe, (y0, x0), axis=(2, 3))
    p = (rolled[:, 0], rolled[:, 1])

    phi = apply_both(fresnel, complex_times(p, t0))
    psi = apply_both(farfield, complex_times(t1, phi))
    part = jnp.sum(psi[0] * psi[0] + psi[1] * psi[1], axis=0)
    resid = (part + swap(part, "cuts")) - measured[0]
    chi = apply_both(conjugate(farfield), (resid[None] * psi[0], resid[None] * psi[1]))
    g1 = jnp.stack([jnp.sum(v, axis=0) for v in conj_times(phi, chi)])
    zeta = apply_both(conjugate(fresnel), conj_times(t1, chi))
    g0 = jnp.stack([jnp.sum(v, axis=0) for v in conj_times(p, zeta)])
    probe_term = jnp.stack(conj_times(t0, zeta), axis=1)
    probe_term = jnp.roll(probe_term, (-y0, -x0), axis=(2, 3))
    grad = jnp.where(first, g0, g1) + swap(jnp.where(first, g1, g0), "cuts")

    rows = length // batches
    sub = row_block // batches
    tile_count = owned.shape[0]
    my_batch, my_tile = lax.axis_index("batch"), lax.axis_index("tile")
    blocks = grad.reshape(2, batches, rows, length).transpose(1, 0, 2, 3)
    blocks = blocks.reshape(batches, 2 * rows, length)
    meta_rows = -(-(3 + groups) // 8) * 8
    start_rows = (y0 - rows * jnp.arange(batches)).astype(jnp.float32)
    spread = lambda v: jnp.broadcast_to(v.astype(jnp.float32), (batches, length))
    meta = [
        spread(jnp.where(cells < x0, slots[1], slots[0])[None]),
        spread(jnp.where(cells < x0, slots[3], slots[2])[None]),
        spread(start_rows[:, None]),
    ]
    meta += [spread(pick[(my_tile - e) % groups][None, None]) for e in range(groups)]
    meta += [jnp.zeros((batches, length), jnp.float32)] * (meta_rows - len(meta))
    messages = jnp.concatenate([blocks, jnp.stack(meta, axis=1)], axis=1)
    probe_rows = 2 * half * sub
    probe_blocks = probe_term.reshape(2 * half, groups, batches, sub, length)
    probe_blocks = probe_blocks.transpose(1, 2, 0, 3, 4).reshape(
        groups, batches, probe_rows, length
    )
    own_objects = lax.dynamic_slice_in_dim(
        owned.reshape(tile_count * 2, batches, rows, length), my_batch, 1, 1
    ).reshape(tile_count * 2, rows, length)
    own_probe = my_probe.reshape(2 * half, groups, batches, sub, length)
    own_probe = lax.dynamic_slice_in_dim(own_probe, my_tile, 1, 1)
    own_probe = lax.dynamic_slice_in_dim(own_probe, my_batch, 1, 2)
    own_probe = own_probe.reshape(probe_rows, length)
    objects_out, probe_out = reduce_and_gather(
        messages, probe_blocks, own_objects, own_probe, batches, groups, rows
    )
    new_objects = objects_out.reshape(objects.shape)
    new_probe = probe_out.reshape(batches, 2 * half, sub, length).transpose(1, 0, 2, 3)
    return (new_objects, new_probe.reshape(half, 2, row_block, length))


def solution(mesh):
    in_specs = (
        P("cuts", "tile", None, None, None),
        P(),
        P(("batch", "tile"), None, None),
        P("batch", "tile", None),
        P(("batch", "tile"), None),
        P(("batch", "tile"), None),
    )
    out_specs = (P("cuts", "tile", None, None, None), P("cuts", None, "tile", None))
    return jax.shard_map(local, mesh=mesh, in_specs=in_specs, out_specs=out_specs, check_vma=False)
```

```python
import functools
import math

import jax
import jax.numpy as jnp
import numpy as np
from jax import lax
from jax.experimental import pallas as pl
from jax.experimental.pallas import tpu as pltpu
from jax.sharding import PartitionSpec as P

EXACT = lax.Precision.HIGHEST
OBJECT_RATE = 0.02
PROBE_RATE = 0.05


def transform_tables(length):
    counter = np.arange(length)
    wave = np.exp(-2j * np.pi / length * (counter[:, None] * counter[None, :] % length))
    signed = np.where(counter < length // 2, counter, counter - length)
    chirp = np.exp(-1j * np.pi / length * (signed * signed % (2 * length)))
    fresnel = (np.conj(wave) * chirp[None, :]) @ wave / length
    unitary = wave / math.sqrt(length)
    as_pair = lambda m: (np.real(m).astype(np.float32), np.imag(m).astype(np.float32))
    return as_pair(fresnel), as_pair(unitary)


def wide_table(matrix):
    re, im = matrix
    return np.concatenate([np.concatenate([re, im], 1), np.concatenate([-im, re], 1)], 0)


def exact_dot(a, b):
    return jnp.dot(a, b, precision=EXACT, preferred_element_type=jnp.float32)


MESH = pl.DeviceIdType.MESH


def step_kernel(
    batches, groups, rows, chunks,
    outg, vec, probe, meas, meta, fres_l, fres_r, far_l, far_r, own_obj, own_prb,
    out_obj, out_prb,
    tin, tt, pp, rot, xin, mid, phi, psi, chi, part, part_in, gg, g_in, pt, msg, prb,
    got, px, ps, py, obj, prn,
    t_send, t_recv, c_send, c_recv,
    g_send, g_recv, f_send, f_recv, x_send, x_recv, y_send, y_recv,
    a_send, a_recv, b_send, b_recv, l_sem,
):
    me, mine, cut = lax.axis_index("batch"), lax.axis_index("tile"), lax.axis_index("cuts")
    depth = batches // 2
    pair = me + 1 - 2 * (me % 2)
    tiles = own_obj.shape[0] // 2
    n = meas.shape[0]
    half = pp.shape[0]
    behind = lambda d: (me + batches - d) % batches

    barrier = pltpu.get_barrier_semaphore()
    for d in range(1, batches):
        pl.semaphore_signal(
            barrier, inc=1, device_id={"batch": (me + d) % batches}, device_id_type=MESH
        )
    for e in range(1, groups):
        pl.semaphore_signal(
            barrier, inc=1, device_id={"tile": (mine + e) % groups}, device_id_type=MESH
        )
    pl.semaphore_signal(barrier, inc=1, device_id={"cuts": 1 - cut}, device_id_type=MESH)
    pl.semaphore_wait(barrier, batches + groups - 1)

    def send(src, dst, sems, place, target):
        copy = pltpu.make_async_remote_copy(
            src_ref=src, dst_ref=dst, send_sem=sems[0].at[place], recv_sem=sems[1].at[place],
            device_id=target, device_id_type=MESH,
        )
        copy.start()
        return copy

    to_batch = lambda d: {"batch": (me + d) % batches}
    to_tile = lambda e: {"tile": (mine + e) % groups}
    other = {"cuts": 1 - cut}
    tile_copies = [
        send(outg.at[(mine + e) % groups], tin.at[e], (t_send, t_recv), e, to_tile(e))
        for e in range(1, groups)
    ]
    tin[0] = outg[mine]

    iota0 = lax.broadcasted_iota(jnp.int32, (n, n), 0).astype(jnp.float32)
    iota1 = lax.broadcasted_iota(jnp.int32, (n, n), 1).astype(jnp.float32)
    size = float(n)
    for k in range(2):
        shift = vec[pl.ds(2 + k, 1), :]
        down = iota1 + shift
        rot[2 * k] = jnp.where(jnp.where(down >= size, down - size, down) == iota0, 1.0, 0.0)
        side = iota0 + shift
        rot[2 * k + 1] = jnp.where(jnp.where(side >= size, side - size, side) == iota1, 1.0, 0.0)
    for m in range(half):
        for c in range(2):
            turned = exact_dot(probe[cut * half + m, c], rot[3])
            pp[m, c] = exact_dot(rot[0], turned)

    def over_rows(step, count=32):
        def body(i, carry):
            step(pl.multiple_of(i * count, count), count)
            return carry

        lax.fori_loop(0, n // count, body, 0)

    for copy in tile_copies:
        copy.wait()

    def choose(r, h):
        row = (lax.broadcasted_iota(jnp.int32, (h, n), 0) + r).astype(jnp.float32)
        slot = jnp.where(row < vec[pl.ds(2, 1), :], vec[pl.ds(1, 1), :], vec[pl.ds(0, 1), :])
        for c in range(2):
            value = jnp.zeros((h, n), jnp.float32)
            for e in range(groups):
                owner = ((mine + groups - e) % groups).astype(jnp.float32)
                value = jnp.where(slot == owner, tin[e, c, pl.ds(r, h), :], value)
            tt[cut, c, pl.ds(r, h), :] = value

    over_rows(choose)
    tile_swap = send(tt.at[cut], tt.at[cut], (c_send, c_recv), 0, other)
    tile_swap.wait()

    def put(m, r, h, re, im):
        xin[pl.ds(m * n + r, h), pl.ds(0, n)] = re
        xin[pl.ds(m * n + r, h), pl.ds(n, n)] = im

    def take(ref, m, r, h):
        spot = pl.ds(m * n, n)
        return ref[pl.ds(r, h), spot], ref[pl.ds(n + r, h), spot]

    def cells(ref, lead, r, h):
        return ref[lead, 0, pl.ds(r, h), :], ref[lead, 1, pl.ds(r, h), :]

    def times(a, b):
        return a[0] * b[0] - a[1] * b[1], a[0] * b[1] + a[1] * b[0]

    def conj_times(a, b):
        return a[0] * b[0] + a[1] * b[1], a[0] * b[1] - a[1] * b[0]

    def transform(left, right, out):
        for m in range(half):
            for c in range(2):
                mid[pl.ds(c * n, n), pl.ds(m * n, n)] = exact_dot(
                    xin[pl.ds(m * n, n), :], right[:, pl.ds(c * n, n)]
                )
        for m in range(half):
            for c in range(2):
                out[pl.ds(c * n, n), pl.ds(m * n, n)] = exact_dot(
                    left[pl.ds(c * n, n), :], mid[:, pl.ds(m * n, n)]
                )

    def enter(r, h):
        for m in range(half):
            put(m, r, h, *times(cells(pp, m, r, h), cells(tt, 0, r, h)))

    over_rows(enter)
    transform(fres_l, fres_r, phi)

    def second(r, h):
        for m in range(half):
            put(m, r, h, *times(cells(tt, 1, r, h), take(phi, m, r, h)))

    over_rows(second)
    transform(far_l, far_r, psi)

    def brightness(r, h):
        total = jnp.zeros((h, n), jnp.float32)
        for m in range(half):
            re, im = take(psi, m, r, h)
            total = total + (re * re + im * im)
        part[pl.ds(r, h), :] = total

    over_rows(brightness)
    part_swap = send(part, part_in, (c_send, c_recv), 1, other)
    part_swap.wait()

    def weigh(r, h):
        rest = part[pl.ds(r, h), :] + part_in[pl.ds(r, h), :] - meas[pl.ds(r, h), :]
        for m in range(half):
            re, im = take(psi, m, r, h)
            put(m, r, h, rest * re, rest * im)

    over_rows(weigh)
    transform(far_r, far_l, chi)

    def back(r, h):
        total = (jnp.zeros((h, n), jnp.float32),) * 2
        for m in range(half):
            wave = take(chi, m, r, h)
            term = conj_times(take(phi, m, r, h), wave)
            total = (total[0] + term[0], total[1] + term[1])
            put(m, r, h, *conj_times(cells(tt, 1, r, h), wave))
        for c in range(2):
            gg[1, c, pl.ds(r, h), :] = total[c]

    over_rows(back)
    transform(fres_r, fres_l, psi)

    def close(r, h):
        total = (jnp.zeros((h, n), jnp.float32),) * 2
        for m in range(half):
            wave = take(psi, m, r, h)
            term = conj_times(cells(pp, m, r, h), wave)
            total = (total[0] + term[0], total[1] + term[1])
            term = conj_times(cells(tt, 0, r, h), wave)
            for c in range(2):
                pt[2 * m + c, pl.ds(r, h), :] = term[c]
        for c in range(2):
            gg[0, c, pl.ds(r, h), :] = total[c]

    over_rows(close)
    grad_swap = send(gg.at[1 - cut], g_in, (c_send, c_recv), 2, other)
    sub = prb.shape[2] // (2 * half)
    for k in range(2 * half):
        turned = exact_dot(rot[1], exact_dot(pt[k], rot[2]))
        for t in range(groups):
            for b in range(batches):
                start = (t * batches + b) * sub
                prb[t, b, pl.ds(k * sub, sub), :] = turned[start : start + sub]
    grad_swap.wait()
    for b in range(batches):
        for c in range(2):
            spot = pl.ds(b * rows, rows)
            msg[b, pl.ds(c * rows, rows), :] = gg[cut, c, spot, :] + g_in[c, spot, :]
        msg[b, pl.ds(2 * rows, meta.shape[1]), :] = meta[b]

    first = {}
    halves = []
    for e in range(1, groups):
        halves.append(
            send(prb.at[(mine + e) % groups], px.at[e], (x_send, x_recv), e, to_tile(e))
        )
    for d in range(1, batches):
        first[d] = send(
            msg.at[(me + d) % batches], got.at[0, d], (g_send, g_recv), d, to_batch(d)
        )
    got[0, 0] = msg[me]
    forwards = []

    def forward(d):
        for e in range(1, groups):
            forwards.append(
                send(got.at[0, d], got.at[e, d], (f_send, f_recv), e * batches + d, to_tile(e))
            )

    forward(0)
    for copy in halves:
        copy.wait()

    def add_probe(b, carry):
        total = prb[mine, b]
        for e in range(1, groups):
            total = total + px[e, b]
        ps[b] = total
        return carry

    lax.fori_loop(0, batches, add_probe, 0)
    probe_sends = [
        send(ps.at[(me + d) % batches], py.at[d], (y_send, y_recv), d, to_batch(d))
        for d in range(1, batches)
    ]
    for d in range(1, batches):
        first[d].wait_recv()
        forward(d)
    for copy in forwards:
        copy.wait()

    mine_f = mine.astype(jnp.float32)
    strips = rows // 8

    def add_strip(i, carry):
        plane, strip = i // strips, i % strips
        start = pl.multiple_of(i * 8, 8)
        row = (lax.broadcasted_iota(jnp.int32, (8, 256), 0) + strip * 8).astype(jnp.float32)
        sums = [jnp.zeros((8, 256), jnp.float32) for _ in range(tiles)]
        for d in range(batches):
            for e in range(groups):
                upper = got[e, d, pl.ds(2 * rows, 1), :]
                lower = got[e, d, pl.ds(2 * rows + 1, 1), :]
                edge = got[e, d, pl.ds(2 * rows + 2, 1), :]
                place = got[0, d, pl.ds(2 * rows + 3 + e, 1), :]
                slot = jnp.where(row < edge, lower, upper)
                value = jnp.where(slot == mine_f, got[e, d, pl.ds(start, 8), :], 0.0)
                for j in range(tiles):
                    sums[j] = sums[j] + jnp.where(place == float(j), value, 0.0)
        spot = pl.multiple_of(strip * 8, 8)
        for j in range(tiles):
            obj[2 * j + plane, pl.ds(spot, 8), :] = (
                own_obj[2 * j + plane, pl.ds(spot, 8), :] - OBJECT_RATE * sums[j]
            )
        return carry

    lax.fori_loop(0, 2 * strips, add_strip, 0)

    locals_ = [pltpu.make_async_copy(obj, out_obj.at[:, me], l_sem.at[0])]
    locals_[0].start()
    part = 2 * tiles // chunks
    pieces = [pl.ds(q * part, part) for q in range(chunks)]
    arriving = {}

    def gather_start(q, src, dst):
        base = q * depth
        arriving[q, 0] = send(src, dst, (a_send, a_recv), base, {"batch": pair})
        for k in range(1, depth):
            arriving[q, k] = send(src, dst, (a_send, a_recv), base + k, to_batch(2 * k))

    for q in range(chunks):
        gather_start(q, obj.at[pieces[q]], out_obj.at[pieces[q], me])

    for copy in probe_sends:
        copy.wait()
    total = ps[me]
    for d in range(1, batches):
        total = total + py[d]
    prn[...] = own_prb[...] - PROBE_RATE / math.sqrt(batches * groups) * total
    locals_.append(pltpu.make_async_copy(prn, out_prb.at[me], l_sem.at[1]))
    locals_[1].start()
    gather_start(chunks, prn, out_prb.at[me])

    relays = []
    for q in range(chunks + 1):
        for k in range(1, depth):
            arriving[q, k].wait_recv()
            b = behind(2 * k)
            ref = out_obj.at[pieces[q], b] if q < chunks else out_prb.at[b]
            relays.append(send(ref, ref, (b_send, b_recv), q * depth + k, {"batch": pair}))
    for q in range(chunks + 1):
        arriving[q, 0].wait_recv()
    for copy in relays:
        copy.wait()
    for copy in arriving.values():
        copy.wait_send()
    for d in range(1, batches):
        first[d].wait_send()
    for copy in locals_:
        copy.wait()


def run_step(outgoing, vectors, probe, measured, meta, own_objects, own_probe, sizes):
    batches, groups, rows, half = sizes
    length = probe.shape[-1]
    fresnel, farfield = transform_tables(length)
    fres_r, far_r = wide_table(fresnel), wide_table(farfield)
    tables = [fres_r.T.copy(), fres_r, far_r.T.copy(), far_r]
    chunks = 4
    depth = batches // 2
    dma = pltpu.SemaphoreType.DMA
    f32 = jnp.float32
    probe_rows = own_probe.shape[0]
    message = (2 * rows + meta.shape[1], length)
    vmem = pl.BlockSpec(memory_space=pltpu.VMEM)
    anywhere = pl.BlockSpec(memory_space=pl.ANY)
    square = (length, length)
    field = (2 * length, half * length)
    return pl.pallas_call(
        functools.partial(step_kernel, batches, groups, rows, chunks),
        out_shape=(
            jax.ShapeDtypeStruct((own_objects.shape[0], batches, rows, length), f32),
            jax.ShapeDtypeStruct((batches, probe_rows, length), f32),
        ),
        in_specs=[vmem] * 11,
        out_specs=(anywhere, anywhere),
        scratch_shapes=[
            pltpu.VMEM((groups, 2) + square, f32),
            pltpu.VMEM((2, 2) + square, f32),
            pltpu.VMEM((half, 2) + square, f32),
            pltpu.VMEM((4,) + square, f32),
            pltpu.VMEM((half * length, 2 * length), f32),
            pltpu.VMEM(field, f32),
            pltpu.VMEM(field, f32),
            pltpu.VMEM(field, f32),
            pltpu.VMEM(field, f32),
            pltpu.VMEM(square, f32),
            pltpu.VMEM(square, f32),
            pltpu.VMEM((2, 2) + square, f32),
            pltpu.VMEM((2,) + square, f32),
            pltpu.VMEM((2 * half,) + square, f32),
            pltpu.VMEM((batches,) + message, f32),
            pltpu.VMEM((groups, batches, probe_rows, length), f32),
            pltpu.VMEM((groups, batches) + message, f32),
            pltpu.VMEM((groups, batches, probe_rows, length), f32),
            pltpu.VMEM((batches, probe_rows, length), f32),
            pltpu.VMEM((batches, probe_rows, length), f32),
            pltpu.VMEM(own_objects.shape, f32),
            pltpu.VMEM(own_probe.shape, f32),
            dma((groups,)), dma((groups,)),
            dma((3,)), dma((3,)),
            dma((batches,)), dma((batches,)),
            dma((groups * batches,)), dma((groups * batches,)),
            dma((groups,)), dma((groups,)),
            dma((batches,)), dma((batches,)),
            dma(((chunks + 1) * depth,)), dma(((chunks + 1) * depth,)),
            dma(((chunks + 1) * depth,)), dma(((chunks + 1) * depth,)),
            dma((2,)),
        ],
        compiler_params=pltpu.CompilerParams(
            collective_id=0, has_side_effects=True, vmem_limit_bytes=56 * 1024 * 1024
        ),
        cost_estimate=pl.CostEstimate(
            flops=14_000_000_000, bytes_accessed=20_000_000, transcendentals=0
        ),
    )(outgoing, vectors, probe, measured, meta, *tables, own_objects, own_probe)


def local(objects, probe, measured, send_list, corner_slot, offsets):
    length = probe.shape[-1]
    half = probe.shape[0] // 2
    groups = lax.axis_size("tile")
    batches = lax.axis_size("batch")
    row_block = length // groups
    cut = lax.axis_index("cuts")
    owned = objects[0]
    pick = send_list[0, 0]
    outgoing = jnp.take(owned, pick, axis=0, mode="clip")
    y0, x0 = offsets[0, 0], offsets[0, 1]
    cells = jnp.arange(length, dtype=jnp.int32)
    slots = corner_slot[0]
    my_probe = lax.dynamic_slice_in_dim(probe, cut * half, half, 0)
    rows = length // batches
    sub = row_block // batches
    tile_count = owned.shape[0]
    my_batch, my_tile = lax.axis_index("batch"), lax.axis_index("tile")
    meta_rows = -(-(3 + groups) // 8) * 8
    upper = jnp.where(cells < x0, slots[1], slots[0])
    lower = jnp.where(cells < x0, slots[3], slots[2])
    as_row = lambda v: jnp.broadcast_to(v.astype(jnp.float32), (length,))
    vectors = jnp.stack([as_row(v) for v in (upper, lower, y0, x0)] + [as_row(0 * y0)] * 4)
    start_rows = y0 - rows * jnp.arange(batches)
    spread = lambda v: jnp.broadcast_to(v.astype(jnp.float32), (batches, length))
    meta = [spread(upper[None]), spread(lower[None]), spread(start_rows[:, None])]
    meta += [spread(pick[(my_tile - e) % groups][None, None]) for e in range(groups)]
    meta += [jnp.zeros((batches, length), jnp.float32)] * (meta_rows - len(meta))
    meta = jnp.stack(meta, axis=1)
    probe_rows = 2 * half * sub
    own_objects = lax.dynamic_slice_in_dim(
        owned.reshape(tile_count * 2, batches, rows, length), my_batch, 1, 1
    ).reshape(tile_count * 2, rows, length)
    own_probe = my_probe.reshape(2 * half, groups, batches, sub, length)
    own_probe = lax.dynamic_slice_in_dim(own_probe, my_tile, 1, 1)
    own_probe = lax.dynamic_slice_in_dim(own_probe, my_batch, 1, 2)
    own_probe = own_probe.reshape(probe_rows, length)
    objects_out, probe_out = run_step(
        outgoing, vectors, probe, measured[0], meta, own_objects, own_probe,
        (batches, groups, rows, half),
    )
    new_objects = objects_out.reshape(objects.shape)
    new_probe = probe_out.reshape(batches, 2 * half, sub, length).transpose(1, 0, 2, 3)
    return (new_objects, new_probe.reshape(half, 2, row_block, length))


def solution(mesh):
    in_specs = (
        P("cuts", "tile", None, None, None),
        P(),
        P(("batch", "tile"), None, None),
        P("batch", "tile", None),
        P(("batch", "tile"), None),
        P(("batch", "tile"), None),
    )
    out_specs = (P("cuts", "tile", None, None, None), P("cuts", None, "tile", None))
    return jax.shard_map(local, mesh=mesh, in_specs=in_specs, out_specs=out_specs, check_vma=False)
```

```python
import functools
import math

import jax
import jax.numpy as jnp
import numpy as np
from jax import lax
from jax.experimental import pallas as pl
from jax.experimental.pallas import tpu as pltpu
from jax.sharding import PartitionSpec as P

EXACT = lax.Precision.HIGHEST
OBJECT_RATE = 0.02
PROBE_RATE = 0.05


def transform_tables(length):
    counter = np.arange(length)
    wave = np.exp(-2j * np.pi / length * (counter[:, None] * counter[None, :] % length))
    signed = np.where(counter < length // 2, counter, counter - length)
    chirp = np.exp(-1j * np.pi / length * (signed * signed % (2 * length)))
    fresnel = (np.conj(wave) * chirp[None, :]) @ wave / length
    unitary = wave / math.sqrt(length)
    as_pair = lambda m: (np.real(m).astype(np.float32), np.imag(m).astype(np.float32))
    return as_pair(fresnel), as_pair(unitary)


def wide_table(matrix):
    re, im = matrix
    return np.concatenate([np.concatenate([re, im], 1), np.concatenate([-im, re], 1)], 0)


def exact_dot(a, b):
    return jnp.dot(a, b, precision=EXACT, preferred_element_type=jnp.float32)


MESH = pl.DeviceIdType.MESH


def step_kernel(
    batches, groups, rows, chunks,
    pick, corner, offs, objs, probe, meas, fres_l, fres_r, far_l, far_r, own_prb,
    out_obj, out_prb,
    outg, tin, tt, pp, rot, xin, mid, phi, psi, chi, part, part_in, gg, g_in, pt, msg, prb,
    got, px, ps, py, obj, prn,
    t_send, t_recv, c_send, c_recv,
    g_send, g_recv, f_send, f_recv, x_send, x_recv, y_send, y_recv,
    a_send, a_recv, b_send, b_recv, l_sem,
):
    me, mine, cut = lax.axis_index("batch"), lax.axis_index("tile"), lax.axis_index("cuts")
    depth = batches // 2
    pair = me + 1 - 2 * (me % 2)
    tiles = objs.shape[0]
    n = meas.shape[0]
    y0, x0 = offs[0], offs[1]
    slots = [corner[k] for k in range(4)]
    half = pp.shape[0]
    behind = lambda d: (me + batches - d) % batches

    def over_rows(step, count=32):
        def body(i, carry):
            step(pl.multiple_of(i * count, count), count)
            return carry

        lax.fori_loop(0, n // count, body, 0)

    barrier = pltpu.get_barrier_semaphore()
    for d in range(1, batches):
        pl.semaphore_signal(
            barrier, inc=1, device_id={"batch": (me + d) % batches}, device_id_type=MESH
        )
    for e in range(1, groups):
        pl.semaphore_signal(
            barrier, inc=1, device_id={"tile": (mine + e) % groups}, device_id_type=MESH
        )
    pl.semaphore_signal(barrier, inc=1, device_id={"cuts": 1 - cut}, device_id_type=MESH)

    def fetch(r, h):
        for t in range(groups):
            for c in range(2):
                outg[t, c, pl.ds(r, h), :] = objs[pick[t], c, pl.ds(r, h), :]

    over_rows(fetch)
    pl.semaphore_wait(barrier, batches + groups - 1)

    def send(src, dst, sems, place, target):
        copy = pltpu.make_async_remote_copy(
            src_ref=src, dst_ref=dst, send_sem=sems[0].at[place], recv_sem=sems[1].at[place],
            device_id=target, device_id_type=MESH,
        )
        copy.start()
        return copy

    to_batch = lambda d: {"batch": (me + d) % batches}
    to_tile = lambda e: {"tile": (mine + e) % groups}
    other = {"cuts": 1 - cut}
    tile_copies = [
        send(outg.at[(mine + e) % groups], tin.at[e], (t_send, t_recv), e, to_tile(e))
        for e in range(1, groups)
    ]
    tin[0] = outg[mine]

    iota0 = lax.broadcasted_iota(jnp.int32, (n, n), 0)
    iota1 = lax.broadcasted_iota(jnp.int32, (n, n), 1)
    for k, shift in enumerate((y0, x0)):
        down, side = iota1 + shift, iota0 + shift
        rot[2 * k] = jnp.where(jnp.where(down >= n, down - n, down) == iota0, 1.0, 0.0)
        rot[2 * k + 1] = jnp.where(jnp.where(side >= n, side - n, side) == iota1, 1.0, 0.0)
    for m in range(half):
        for c in range(2):
            turned = exact_dot(probe[cut * half + m, c], rot[3])
            pp[m, c] = exact_dot(rot[0], turned)

    for copy in tile_copies:
        copy.wait()

    def choose(r, h):
        low = lax.broadcasted_iota(jnp.int32, (h, n), 0) + r < y0
        side = lax.broadcasted_iota(jnp.int32, (h, n), 1) < x0
        slot = jnp.where(
            low, jnp.where(side, slots[3], slots[2]), jnp.where(side, slots[1], slots[0])
        )
        for c in range(2):
            value = jnp.zeros((h, n), jnp.float32)
            for e in range(groups):
                owner = (mine + groups - e) % groups
                value = jnp.where(slot == owner, tin[e, c, pl.ds(r, h), :], value)
            tt[cut, c, pl.ds(r, h), :] = value

    over_rows(choose)
    tile_swap = send(tt.at[cut], tt.at[cut], (c_send, c_recv), 0, other)
    tile_swap.wait()

    def put(m, r, h, re, im):
        xin[pl.ds(m * n + r, h), pl.ds(0, n)] = re
        xin[pl.ds(m * n + r, h), pl.ds(n, n)] = im

    def take(ref, m, r, h):
        spot = pl.ds(m * n, n)
        return ref[pl.ds(r, h), spot], ref[pl.ds(n + r, h), spot]

    def cells(ref, lead, r, h):
        return ref[lead, 0, pl.ds(r, h), :], ref[lead, 1, pl.ds(r, h), :]

    def times(a, b):
        return a[0] * b[0] - a[1] * b[1], a[0] * b[1] + a[1] * b[0]

    def conj_times(a, b):
        return a[0] * b[0] + a[1] * b[1], a[0] * b[1] - a[1] * b[0]

    def transform(left, right, out):
        for m in range(half):
            for c in range(2):
                mid[pl.ds(c * n, n), pl.ds(m * n, n)] = exact_dot(
                    xin[pl.ds(m * n, n), :], right[:, pl.ds(c * n, n)]
                )
        for m in range(half):
            for c in range(2):
                out[pl.ds(c * n, n), pl.ds(m * n, n)] = exact_dot(
                    left[pl.ds(c * n, n), :], mid[:, pl.ds(m * n, n)]
                )

    def enter(r, h):
        for m in range(half):
            put(m, r, h, *times(cells(pp, m, r, h), cells(tt, 0, r, h)))

    over_rows(enter)
    transform(fres_l, fres_r, phi)

    def second(r, h):
        for m in range(half):
            put(m, r, h, *times(cells(tt, 1, r, h), take(phi, m, r, h)))

    over_rows(second)
    transform(far_l, far_r, psi)

    def brightness(r, h):
        total = jnp.zeros((h, n), jnp.float32)
        for m in range(half):
            re, im = take(psi, m, r, h)
            total = total + (re * re + im * im)
        part[pl.ds(r, h), :] = total

    over_rows(brightness)
    part_swap = send(part, part_in, (c_send, c_recv), 1, other)
    part_swap.wait()

    def weigh(r, h):
        rest = part[pl.ds(r, h), :] + part_in[pl.ds(r, h), :] - meas[pl.ds(r, h), :]
        for m in range(half):
            re, im = take(psi, m, r, h)
            put(m, r, h, rest * re, rest * im)

    over_rows(weigh)
    transform(far_r, far_l, chi)

    def back(r, h):
        total = (jnp.zeros((h, n), jnp.float32),) * 2
        for m in range(half):
            wave = take(chi, m, r, h)
            term = conj_times(take(phi, m, r, h), wave)
            total = (total[0] + term[0], total[1] + term[1])
            put(m, r, h, *conj_times(cells(tt, 1, r, h), wave))
        for c in range(2):
            gg[1, c, pl.ds(r, h), :] = total[c]

    over_rows(back)
    transform(fres_r, fres_l, psi)

    def close(r, h):
        total = (jnp.zeros((h, n), jnp.float32),) * 2
        for m in range(half):
            wave = take(psi, m, r, h)
            term = conj_times(cells(pp, m, r, h), wave)
            total = (total[0] + term[0], total[1] + term[1])
            term = conj_times(cells(tt, 0, r, h), wave)
            for c in range(2):
                pt[2 * m + c, pl.ds(r, h), :] = term[c]
        for c in range(2):
            gg[0, c, pl.ds(r, h), :] = total[c]

    over_rows(close)
    grad_swap = send(gg.at[1 - cut], g_in, (c_send, c_recv), 2, other)
    sub = prb.shape[2] // (2 * half)
    for k in range(2 * half):
        turned = exact_dot(rot[1], exact_dot(pt[k], rot[2]))
        for t in range(groups):
            for b in range(batches):
                start = (t * batches + b) * sub
                prb[t, b, pl.ds(k * sub, sub), :] = turned[start : start + sub]
    meta_rows = msg.shape[1] - 2 * rows
    real = lambda v: v.astype(jnp.float32)
    line = lax.broadcasted_iota(jnp.int32, (meta_rows, n), 0)
    side = lax.broadcasted_iota(jnp.int32, (meta_rows, n), 1) < x0
    upper = jnp.where(side, real(slots[1]), real(slots[0]))
    lower = jnp.where(side, real(slots[3]), real(slots[2]))
    meta = jnp.where(line == 0, upper, lower)
    for e in range(groups):
        meta = jnp.where(line == 3 + e, real(pick[(mine + groups - e) % groups]), meta)
    grad_swap.wait()
    for b in range(batches):
        for c in range(2):
            spot = pl.ds(b * rows, rows)
            msg[b, pl.ds(c * rows, rows), :] = gg[cut, c, spot, :] + g_in[c, spot, :]
        msg[b, pl.ds(2 * rows, meta_rows), :] = jnp.where(line == 2, real(y0 - rows * b), meta)

    first = {}
    halves = []
    for e in range(1, groups):
        halves.append(
            send(prb.at[(mine + e) % groups], px.at[e], (x_send, x_recv), e, to_tile(e))
        )
    for d in range(1, batches):
        first[d] = send(
            msg.at[(me + d) % batches], got.at[0, d], (g_send, g_recv), d, to_batch(d)
        )
    got[0, 0] = msg[me]
    forwards = []

    def forward(d):
        for e in range(1, groups):
            forwards.append(
                send(got.at[0, d], got.at[e, d], (f_send, f_recv), e * batches + d, to_tile(e))
            )

    forward(0)
    for copy in halves:
        copy.wait()

    def add_probe(b, carry):
        total = prb[mine, b]
        for e in range(1, groups):
            total = total + px[e, b]
        ps[b] = total
        return carry

    lax.fori_loop(0, batches, add_probe, 0)
    probe_sends = [
        send(ps.at[(me + d) % batches], py.at[d], (y_send, y_recv), d, to_batch(d))
        for d in range(1, batches)
    ]
    for d in range(1, batches):
        first[d].wait_recv()
        forward(d)
    for copy in forwards:
        copy.wait()

    mine_f = mine.astype(jnp.float32)
    strips = rows // 8

    def add_strip(i, carry):
        plane, strip = i // strips, i % strips
        start = pl.multiple_of(i * 8, 8)
        row = (lax.broadcasted_iota(jnp.int32, (8, 256), 0) + strip * 8).astype(jnp.float32)
        sums = [jnp.zeros((8, 256), jnp.float32) for _ in range(tiles)]
        for d in range(batches):
            for e in range(groups):
                upper = got[e, d, pl.ds(2 * rows, 1), :]
                lower = got[e, d, pl.ds(2 * rows + 1, 1), :]
                edge = got[e, d, pl.ds(2 * rows + 2, 1), :]
                place = got[0, d, pl.ds(2 * rows + 3 + e, 1), :]
                slot = jnp.where(row < edge, lower, upper)
                value = jnp.where(slot == mine_f, got[e, d, pl.ds(start, 8), :], 0.0)
                for j in range(tiles):
                    sums[j] = sums[j] + jnp.where(place == float(j), value, 0.0)
        spot = pl.multiple_of(strip * 8, 8)
        here = pl.multiple_of(me * rows + strip * 8, 8)
        for j in range(tiles):
            obj[2 * j + plane, pl.ds(spot, 8), :] = (
                objs[j, plane, pl.ds(here, 8), :] - OBJECT_RATE * sums[j]
            )
        return carry

    lax.fori_loop(0, 2 * strips, add_strip, 0)

    locals_ = [pltpu.make_async_copy(obj, out_obj.at[:, me], l_sem.at[0])]
    locals_[0].start()
    part = 2 * tiles // chunks
    pieces = [pl.ds(q * part, part) for q in range(chunks)]
    arriving = {}

    def gather_start(q, src, dst):
        base = q * depth
        arriving[q, 0] = send(src, dst, (a_send, a_recv), base, {"batch": pair})
        for k in range(1, depth):
            arriving[q, k] = send(src, dst, (a_send, a_recv), base + k, to_batch(2 * k))

    for q in range(chunks):
        gather_start(q, obj.at[pieces[q]], out_obj.at[pieces[q], me])

    for copy in probe_sends:
        copy.wait()
    total = ps[me]
    for d in range(1, batches):
        total = total + py[d]
    prn[...] = own_prb[...] - PROBE_RATE / math.sqrt(batches * groups) * total
    locals_.append(pltpu.make_async_copy(prn, out_prb.at[me], l_sem.at[1]))
    locals_[1].start()
    gather_start(chunks, prn, out_prb.at[me])

    relays = []
    for q in range(chunks + 1):
        for k in range(1, depth):
            arriving[q, k].wait_recv()
            b = behind(2 * k)
            ref = out_obj.at[pieces[q], b] if q < chunks else out_prb.at[b]
            relays.append(send(ref, ref, (b_send, b_recv), q * depth + k, {"batch": pair}))
    for q in range(chunks + 1):
        arriving[q, 0].wait_recv()
    for copy in relays:
        copy.wait()
    for copy in arriving.values():
        copy.wait_send()
    for d in range(1, batches):
        first[d].wait_send()
    for copy in locals_:
        copy.wait()


def run_step(pick, corner, offset, owned, probe, measured, own_probe, sizes):
    batches, groups, rows, half = sizes
    length = probe.shape[-1]
    fresnel, farfield = transform_tables(length)
    fres_r, far_r = wide_table(fresnel), wide_table(farfield)
    tables = [fres_r.T.copy(), fres_r, far_r.T.copy(), far_r]
    chunks = 4
    depth = batches // 2
    dma = pltpu.SemaphoreType.DMA
    f32 = jnp.float32
    probe_rows = own_probe.shape[0]
    message = (2 * rows - (-(3 + groups) // 8) * 8, length)
    block = (2 * owned.shape[0], rows, length)
    smem = pl.BlockSpec(memory_space=pltpu.SMEM)
    vmem = pl.BlockSpec(memory_space=pltpu.VMEM)
    anywhere = pl.BlockSpec(memory_space=pl.ANY)
    square = (length, length)
    field = (2 * length, half * length)
    return pl.pallas_call(
        functools.partial(step_kernel, batches, groups, rows, chunks),
        out_shape=(
            jax.ShapeDtypeStruct((block[0], batches, rows, length), f32),
            jax.ShapeDtypeStruct((batches, probe_rows, length), f32),
        ),
        in_specs=[smem] * 3 + [vmem] * 8,
        out_specs=(anywhere, anywhere),
        scratch_shapes=[
            pltpu.VMEM((groups, 2) + square, f32),
            pltpu.VMEM((groups, 2) + square, f32),
            pltpu.VMEM((2, 2) + square, f32),
            pltpu.VMEM((half, 2) + square, f32),
            pltpu.VMEM((4,) + square, f32),
            pltpu.VMEM((half * length, 2 * length), f32),
            pltpu.VMEM(field, f32),
            pltpu.VMEM(field, f32),
            pltpu.VMEM(field, f32),
            pltpu.VMEM(field, f32),
            pltpu.VMEM(square, f32),
            pltpu.VMEM(square, f32),
            pltpu.VMEM((2, 2) + square, f32),
            pltpu.VMEM((2,) + square, f32),
            pltpu.VMEM((2 * half,) + square, f32),
            pltpu.VMEM((batches,) + message, f32),
            pltpu.VMEM((groups, batches, probe_rows, length), f32),
            pltpu.VMEM((groups, batches) + message, f32),
            pltpu.VMEM((groups, batches, probe_rows, length), f32),
            pltpu.VMEM((batches, probe_rows, length), f32),
            pltpu.VMEM((batches, probe_rows, length), f32),
            pltpu.VMEM(block, f32),
            pltpu.VMEM(own_probe.shape, f32),
            dma((groups,)), dma((groups,)),
            dma((3,)), dma((3,)),
            dma((batches,)), dma((batches,)),
            dma((groups * batches,)), dma((groups * batches,)),
            dma((groups,)), dma((groups,)),
            dma((batches,)), dma((batches,)),
            dma(((chunks + 1) * depth,)), dma(((chunks + 1) * depth,)),
            dma(((chunks + 1) * depth,)), dma(((chunks + 1) * depth,)),
            dma((2,)),
        ],
        compiler_params=pltpu.CompilerParams(
            collective_id=0, has_side_effects=True, vmem_limit_bytes=44 * 1024 * 1024
        ),
        cost_estimate=pl.CostEstimate(
            flops=14_000_000_000, bytes_accessed=20_000_000, transcendentals=0
        ),
    )(pick, corner, offset, owned, probe, measured, *tables, own_probe)


def local(objects, probe, measured, send_list, corner_slot, offsets):
    length = probe.shape[-1]
    half = probe.shape[0] // 2
    groups = lax.axis_size("tile")
    batches = lax.axis_size("batch")
    row_block = length // groups
    cut = lax.axis_index("cuts")
    owned = objects[0]
    pick = send_list[0, 0]
    rows = length // batches
    sub = row_block // batches
    zero = jnp.zeros((), jnp.int32)
    own_probe = lax.dynamic_slice(
        probe.reshape(4 * half, groups, batches, sub, length),
        (cut * 2 * half, lax.axis_index("tile"), lax.axis_index("batch"), zero, zero),
        (2 * half, 1, 1, sub, length),
    ).reshape(2 * half * sub, length)
    objects_out, probe_out = run_step(
        pick, corner_slot[0], offsets[0], owned, probe, measured[0], own_probe,
        (batches, groups, rows, half),
    )
    new_objects = objects_out.reshape(objects.shape)
    new_probe = probe_out.reshape(batches, 2 * half, sub, length).transpose(1, 0, 2, 3)
    return (new_objects, new_probe.reshape(half, 2, row_block, length))


def solution(mesh):
    in_specs = (
        P("cuts", "tile", None, None, None),
        P(),
        P(("batch", "tile"), None, None),
        P("batch", "tile", None),
        P(("batch", "tile"), None),
        P(("batch", "tile"), None),
    )
    out_specs = (P("cuts", "tile", None, None, None), P("cuts", None, "tile", None))
    return jax.shard_map(local, mesh=mesh, in_specs=in_specs, out_specs=out_specs, check_vma=False)
```
